256 devices in a mesh: tm: 64 (over z, y, core), sub: 4 (over x).
Axes of the slice: x: 4, y: 4, z: 8, core: 2. Of those that a mesh axis runs over, the one named last changes fastest.
Arguments:
- transition: float32 [512, 256, 256], P(('tm', 'sub')), may hold values from -1 to 2
- precision: float32 [512, 256], P(('tm', 'sub')), may hold values from 4e-05 to 1.01
- info: float32 [512, 256, 128], P(('tm', 'sub')), may hold values from -2 to 2
Outputs:
- smoothed: float32 [512, 256, 128], P(('tm', 'sub'))
The draws below stay inside these ranges and needn't reach their ends.
All inputs are finite; a program needn't handle non-finite values.
Results may differ from the reference program's by a relative error of at most 0.0027.
Values sent between devices are 32-bit elements; how exact they have to be, the bound alone decides.
A program may use at most 128 MiB of HBM per device.

```python
import math
import jax
import jax.numpy as jnp
from jax import lax

STATES = 256
RHS = 128
STEPS = 512


def slow_flags(key):
    order = jax.random.permutation(jax.random.fold_in(key, 5), STATES)
    return (order < STATES // 2).astype(jnp.float32)


def draw_transition(key, part):
    slow = slow_flags(key)
    observed = 1.0 - slow
    noise_key = jax.random.fold_in(key, 11)
    noise = jnp.clip(jax.random.normal(noise_key, (STEPS, STATES, STATES), jnp.float32), -4.0, 4.0)
    coupling = 0.3 * observed[:, None] * observed[None, :] + 0.1 * slow[:, None] * observed[None, :] + 0.05 * slow[:, None] * slow[None, :]
    identity = jnp.eye(STATES, dtype=jnp.float32)
    return identity[None] + coupling[None] * noise / math.sqrt(STATES)


def draw_precision(key, part):
    slow = slow_flags(key)
    level = jax.random.uniform(jax.random.fold_in(key, 21), (STEPS, STATES), jnp.float32)
    observed_value = 0.02 * jnp.exp(level * math.log(50.0))
    slow_value = 5e-05 * jnp.exp(level * math.log(4.0))
    return slow[None, :] * slow_value + (1.0 - slow[None, :]) * observed_value


def draw_info(key, part):
    slow = slow_flags(key)
    spread = 0.002 * slow + 0.5 * (1.0 - slow)
    rough_key = jax.random.fold_in(key, 31)
    rough = jnp.clip(jax.random.normal(rough_key, (STEPS, STATES, RHS), jnp.float32), -3.0, 3.0)
    return spread[None, :, None] * rough


def setup_inputs(seed: int = 0) -> dict:
    key_list = jax.random.split(jax.random.key(seed), 4)
    transition = draw_transition(jax.random.fold_in(key_list[3], 71), 0)
    precision = draw_precision(jax.random.fold_in(key_list[3], 71), 0)
    info = draw_info(jax.random.fold_in(key_list[3], 71), 0)
    return {"transition": transition, "precision": precision, "info": info}


def solve_with(factor, right_side):
    return jax.scipy.linalg.cho_solve((factor, True), right_side)

def reference(transition, precision, info):
    highest = lax.Precision.HIGHEST
    identity = jnp.eye(STATES, dtype=jnp.float32)
    zero_block = jnp.zeros((1, STATES, STATES), jnp.float32)
    successors = jnp.concatenate([transition[1:], zero_block], 0)
    couplings = jnp.concatenate([zero_block, transition[1:]], 0)
    diagonal = identity[None] + identity[None] * precision[:, None, :] + jnp.einsum('tji,tjk->tik', successors, successors, precision=highest)

    def forward(state_pair, inputs):
        factor_prev, remainder_prev = state_pair
        diag_block, coupling, source = inputs
        solved = solve_with(factor_prev, jnp.concatenate([coupling.T, remainder_prev], 1))
        product = jnp.dot(coupling, solved, precision=highest)
        schur_block = diag_block - product[:, :STATES]
        remainder = source + product[:, STATES:]
        factor = jnp.linalg.cholesky(schur_block)
        return ((factor, remainder), (factor, remainder))
    initial = (identity, jnp.zeros((STATES, RHS), jnp.float32))
    last_pair, stacked = lax.scan(forward, initial, (diagonal, couplings, info))
    factors, remainders = stacked

    def backward(later_values, inputs):
        factor, remainder, coupling = inputs
        values_now = solve_with(factor, remainder + jnp.dot(coupling.T, later_values, precision=highest))
        return (values_now, values_now)
    first_values, solution = lax.scan(backward, jnp.zeros((STATES, RHS), jnp.float32), (factors, remainders, successors), reverse=True)
    return solution
```

```python
import functools

import jax
import jax.numpy as jnp
from jax import lax
from jax.experimental import pallas as pl
from jax.experimental.pallas import tpu as pltpu
from jax.sharding import PartitionSpec as P

HIGHEST = lax.Precision.HIGHEST
F32 = jnp.float32
N = 256
H = 128
RHS = 128
WIDE = 4 * N
VWIDE = 2 * N + RHS
J0, D0, M0, L0, R0 = 0, N, 2 * N, 3 * N, 3 * N + RHS


def mul(a, b):
    return jnp.dot(a, b, precision=HIGHEST, preferred_element_type=F32)


def mul_tn(a, b):
    return lax.dot_general(a, b, (((0,), (0,)), ((), ())), precision=HIGHEST, preferred_element_type=F32)


def row_of(q, s):
    return jnp.broadcast_to(q[s : s + 1, :], (8, H))


def column_of(q, j):
    return jnp.broadcast_to(q[:, j : j + 1], (8, H))


def inverse_half(block):
    rows = [block[8 * i : 8 * i + 8, :] for i in range(H // 8)]
    lane = lax.broadcasted_iota(jnp.int32, (8, H), 1)
    sub = lax.broadcasted_iota(jnp.int32, (8, H), 0)
    count = len(rows)
    for k in range(count):
        base = 8 * k
        inside = (lane >= base) & (lane < base + 8)
        panel = rows[k]
        cols = [column_of(panel, base + j) for j in range(8)]
        panel = jnp.where(inside, jnp.where(lane - base == sub, 1.0, 0.0), panel)
        for s in (0, 2, 4, 6):
            x, y = cols[s], cols[s + 1]
            a, b, d = row_of(x, s), row_of(y, s), row_of(y, s + 1)
            r = 1.0 / (a * d - b * b)
            first, pair = sub == s, (sub == s) | (sub == s + 1)

            def step(q):
                q0, q1 = row_of(q, s), row_of(q, s + 1)
                n0 = (d * q0 - b * q1) * r
                n1 = (a * q1 - b * q0) * r
                return jnp.where(pair, jnp.where(first, n0, n1), q - (x * n0 + y * n1))

            for j in range(s + 2, 8):
                cols[j] = step(cols[j])
            panel = step(panel)
        lead = [row_of(panel, j) for j in range(8)]
        for i in list(range(k + 1, count)) + list(range(k)):
            q = rows[i]
            m = [column_of(q, base + j) * lead[j] for j in range(8)]
            total = ((m[0] + m[1]) + (m[2] + m[3])) + ((m[4] + m[5]) + (m[6] + m[7]))
            rows[i] = jnp.where(inside, 0.0, q) - total
        rows[k] = panel
    return jnp.concatenate(rows, 0)


def solve_spd(a11, a12, a22, g1, g2):
    x11 = inverse_half(a11)
    w = mul(x11, a12)
    schur = a22 - mul_tn(a12, w)
    z1 = mul(x11, g1)
    rest = g2 - mul_tn(a12, z1)
    v2 = mul(inverse_half(schur), rest)
    return z1 - mul(w, v2), v2


def pick(flag, a, b):
    return jnp.where(flag, a, b)


def merge_kernel(flags, own, got, out, v):
    left, next_left = flags[0] == 0, flags[1] == 0
    d = pick(left, own[:, D0 : D0 + N] + got[:, J0 : J0 + N], own[:, J0 : J0 + N] + got[:, D0 : D0 + N])
    sb = pick(left, own[:, R0:] + got[:, L0:R0], own[:, L0:R0] + got[:, R0:])
    m_own, m_got = own[:, M0:L0], got[:, M0:L0]
    g1, g2 = pick(left, m_own, m_got), pick(left, m_got, m_own)
    g = jnp.concatenate([g1, g2, sb], 1)
    v1, v2 = solve_spd(d[:H, :H], d[:H, H:], d[H:, H:], g[:H], g[H:])
    v[:H, :] = v1
    v[H:, :] = v2
    va, vc, vs = v[:, :N], v[:, N : 2 * N], v[:, 2 * N :]
    j1, d2 = pick(left, own[:, :N], got[:, :N]), pick(left, got[:, D0:M0], own[:, D0:M0])
    l1, r2 = pick(left, own[:, L0:R0], got[:, L0:R0]), pick(left, got[:, R0:], own[:, R0:])
    out[:, :N] = j1 - mul_tn(g1, va)
    out[:, D0:M0] = d2 - mul_tn(g2, vc)
    out[:, M0:L0] = -mul_tn(pick(next_left, g2, g1), pick(next_left, va, vc))
    out[:, L0:R0] = l1 - mul_tn(g1, vs)
    out[:, R0:] = r2 - mul_tn(g2, vs)


def diag_of(row):
    i = lax.broadcasted_iota(jnp.int32, (N, N), 0)
    j = lax.broadcasted_iota(jnp.int32, (N, N), 1)
    return jnp.where(i == j, jnp.broadcast_to(row, (N, N)), 0.0)


def column_from(row):
    i = lax.broadcasted_iota(jnp.int32, (N, N), 0)
    j = lax.broadcasted_iota(jnp.int32, (N, N), 1)
    return jnp.sum(jnp.where(i == j, jnp.broadcast_to(row, (N, N)), 0.0), 1, keepdims=True)


def first_kernel(flags, f, p, info, out, v):
    next_left, is_first, is_last = flags[1] == 0, flags[2] == 1, flags[3] == 1
    f1 = pick(is_first, jnp.zeros((N, N), F32), f[0])
    f2 = f[1]
    p1, p2 = p[0:1, :], p[1:2, :]
    own_p2 = column_from(p2)
    weight = pick(is_last, own_p2 / (1.0 + own_p2), jnp.ones((N, 1), F32))
    j2 = mul_tn(f2, f2 * weight)
    d = diag_of(1.0 + p1) + j2
    tail = mul_tn(f2, info[1] / (1.0 + own_p2))
    sb = info[0] + pick(is_last, tail, jnp.zeros_like(tail))
    g1 = -f1
    g2 = pick(is_last, jnp.zeros((N, N), F32), -f2.T)
    g = jnp.concatenate([g1, g2, sb], 1)
    v1, v2 = solve_spd(d[:H, :H], d[:H, H:], d[H:, H:], g[:H], g[H:])
    v[:H, :] = v1
    v[H:, :] = v2
    va, vc, vs = v[:, :N], v[:, N : 2 * N], v[:, 2 * N :]
    out[:, :N] = mul_tn(g1, g1 - va)
    out[:, D0:M0] = diag_of(pick(is_last, jnp.ones_like(p2), 1.0 + p2)) - mul_tn(g2, vc)
    out[:, M0:L0] = -mul_tn(pick(next_left, g2, g1), pick(next_left, va, vc))
    out[:, L0:R0] = -mul_tn(g1, vs)
    out[:, R0:] = pick(is_last, jnp.zeros((N, RHS), F32), info[1]) - mul_tn(g2, vs)


def top_kernel(flags, own, got, out):
    left = flags[0] == 0
    d = pick(left, own[:, D0 : D0 + N] + got[:, J0 : J0 + N], own[:, J0 : J0 + N] + got[:, D0 : D0 + N])
    sb = pick(left, own[:, R0:] + got[:, L0:R0], own[:, L0:R0] + got[:, R0:])
    v1, v2 = solve_spd(d[:H, :H], d[:H, H:], d[H:, H:], sb[:H], sb[H:])
    out[:H, :] = v1
    out[H:, :] = v2


def back_kernel(bits, depth, f, p, info, top, *refs):
    vs, out = refs[:-1], refs[-1]
    is_last = bits[depth] == 1
    zero = jnp.zeros((N, RHS), F32)
    left = bits[depth - 1] == 0
    a, c = pick(left, zero, top[...]), pick(left, top[...], zero)
    for k in range(depth - 2, -1, -1):
        v = vs[k + 1]
        b = v[:, 2 * N :] - mul(v[:, :N], a) - mul(v[:, N : 2 * N], c)
        left = bits[k] == 0
        a, c = pick(left, a, b), pick(left, b, c)
    v = vs[0]
    b = v[:, 2 * N :] - mul(v[:, :N], a) - mul(v[:, N : 2 * N], c)
    out[0] = b
    end = (info[1] + mul(f[1], b)) / (1.0 + column_from(p[1:2, :]))
    out[1] = pick(is_last, end, c)


SMEM = pl.BlockSpec(memory_space=pltpu.SMEM)
VMEM = pl.BlockSpec(memory_space=pltpu.VMEM)
PARAMS = pltpu.CompilerParams(vmem_limit_bytes=48 * 1024 * 1024)


def shape(*dims):
    return jax.ShapeDtypeStruct(dims, F32)


def shards(transition, precision, info):
    sub_size = lax.axis_size("sub")
    devices = lax.axis_size("tm") * sub_size
    depth = devices.bit_length() - 1
    me = lax.axis_index("tm") * sub_size + lax.axis_index("sub")
    bits = [lax.rem(lax.div(me, 2**k), 2) for k in range(depth)] + [(me == devices - 1).astype(jnp.int32)]
    is_first, is_last = (me == 0).astype(jnp.int32), bits[depth]

    def flags(k):
        return jnp.stack([bits[max(k, 0)], bits[k + 1], is_first, is_last])

    element, v = pl.pallas_call(
        first_kernel,
        out_shape=(shape(N, WIDE), shape(N, VWIDE)),
        in_specs=[SMEM, VMEM, VMEM, VMEM],
        out_specs=(VMEM, VMEM),
        compiler_params=PARAMS,
        name="first",
    )(flags(-1), transition, precision, info)
    kept = [v]
    for k in range(depth):
        pairs = [(i, i ^ 2**k) for i in range(devices)]
        got = lax.ppermute(element, ("tm", "sub"), pairs)
        if k < depth - 1:
            element, v = pl.pallas_call(
                merge_kernel,
                out_shape=(shape(N, WIDE), shape(N, VWIDE)),
                in_specs=[SMEM, VMEM, VMEM],
                out_specs=(VMEM, VMEM),
                compiler_params=PARAMS,
                name="merge",
            )(flags(k), element, got)
            kept.append(v)
        else:
            top = pl.pallas_call(
                top_kernel,
                out_shape=shape(N, RHS),
                in_specs=[SMEM, VMEM, VMEM],
                out_specs=VMEM,
                compiler_params=PARAMS,
                name="top",
            )(flags(k), element, got)

    def back(bits_ref, *refs):
        back_kernel(bits_ref, depth, *refs)

    return pl.pallas_call(
        back,
        out_shape=shape(2, N, RHS),
        in_specs=[SMEM] + [VMEM] * (4 + len(kept)),
        out_specs=VMEM,
        compiler_params=PARAMS,
        name="back",
    )(jnp.stack(bits), transition, precision, info, top, *kept)


def solution(mesh):
    placed = (P(("tm", "sub"), None, None), P(("tm", "sub"), None), P(("tm", "sub"), None, None))
    return jax.shard_map(
        shards, mesh=mesh, in_specs=placed, out_specs=P(("tm", "sub"), None, None), check_vma=False
    )
```

```python
import jax
import jax.numpy as jnp
from jax import lax
from jax.experimental import pallas as pl
from jax.experimental.pallas import tpu as pltpu
from jax.sharding import PartitionSpec as P

HIGHEST = lax.Precision.HIGHEST
F32 = jnp.float32
N = 256
H = 128
RHS = 128
DEPTH = 8
DIRECT = 3
M0, C0, O0, E0, WIDE = N, 2 * N, 2 * N + RHS, 3 * N + RHS, 4 * N
PARTS = ((64, 0, H), (128, H, H), (128, M0, N + RHS), (64, O0, H), (128, O0 + H, H + RHS))


def mul(a, b):
    return jnp.dot(a, b, precision=HIGHEST, preferred_element_type=F32)


def mul_tn(a, b):
    return lax.dot_general(a, b, (((0,), (0,)), ((), ())), precision=HIGHEST, preferred_element_type=F32)


def mul_nt(a, b):
    return lax.dot_general(a, b, (((1,), (1,)), ((), ())), precision=HIGHEST, preferred_element_type=F32)


def eliminate_panel(panel, base, lane, sub):
    cols = [jnp.broadcast_to(panel[:, base + j : base + j + 1], (8, H)) for j in range(8)]
    panel = jnp.where((lane >= base) & (lane < base + 8), jnp.where(lane - base == sub, 1.0, 0.0), panel)
    for s in (0, 2, 4, 6):
        x, y = cols[0], cols[1]
        a, b, d = (jnp.broadcast_to(q[i : i + 1, :], (8, H)) for q, i in ((x, s), (y, s), (y, s + 1)))
        r = 1.0 / (a * d - b * b)
        first, pair = sub == s, (sub == s) | (sub == s + 1)
        u = jnp.where(pair, jnp.where(first, d, -b), y * b - x * d) * r
        w = jnp.where(pair, jnp.where(first, -b, a), x * b - y * a) * r
        m = 7 - s
        wide = jnp.concatenate(cols[2:] + [panel], 1)
        q0 = jnp.broadcast_to(wide[s : s + 1, :], wide.shape)
        q1 = jnp.broadcast_to(wide[s + 1 : s + 2, :], wide.shape)
        keep = jnp.where(pair, 0.0, 1.0)
        keep, u, w = (jnp.concatenate([z] * m, 1) for z in (keep, u, w))
        wide = keep * wide + (u * q0 + w * q1)
        cols = [wide[:, H * j : H * j + H] for j in range(m - 1)]
        panel = wide[:, H * (m - 1) :]
    return panel


def inverse_half(a, middle=None):
    lane = lax.broadcasted_iota(jnp.int32, (8, H), 1)
    sub = lax.broadcasted_iota(jnp.int32, (8, H), 0)
    lanes = lax.broadcasted_iota(jnp.int32, (H, H), 1)
    for k in range(H // 8):
        if k == 8 and middle is not None:
            middle()
        base = 8 * k
        panel = eliminate_panel(a[base : base + 8, :], base, lane, sub)
        m = [
            jnp.broadcast_to(a[:, base + j : base + j + 1], (H, H)) * jnp.broadcast_to(panel[j : j + 1, :], (H, H))
            for j in range(8)
        ]
        total = ((m[0] + m[1]) + (m[2] + m[3])) + ((m[4] + m[5]) + (m[6] + m[7]))
        new = jnp.where((lanes >= base) & (lanes < base + 8), 0.0, a) - total
        parts = ([new[:base, :]] if k else []) + [panel] + ([new[base + 8 :, :]] if k < H // 8 - 1 else [])
        a = jnp.concatenate(parts, 0)
    return a


def on_diagonal():
    return lax.broadcasted_iota(jnp.int32, (N, N), 0) == lax.broadcasted_iota(jnp.int32, (N, N), 1)


def diag_of(row):
    return jnp.where(on_diagonal(), jnp.broadcast_to(row, (N, N)), 0.0)


def column_from(row):
    return jnp.sum(diag_of(row), 1, keepdims=True)


def kernel(f, p, info, out, el, vb, vs, ends, inv, send_sem, recv_sem, pass_sem):
    tm, x = lax.axis_index("tm"), lax.axis_index("sub")
    me = tm * 4 + x
    core, y, z = tm % 2, (tm // 2) % 4, tm // 8
    last = 2 ** DEPTH - 1

    def place(x, core, y, z):
        return (z * 4 + y) * 2 + core, x

    def other(q):
        return q + 1 - 2 * (q % 2)

    partners = [
        place(other(x), core, y, z),
        place(3 - x, core, y, z),
        place(x, 1 - core, y, z),
        place(x, core, other(y), z),
        place(x, core, 3 - y, z),
        place(x, core, y, other(z)),
        place(x, core, y, z + 2 - 4 * ((z // 2) % 2)),
        place(x, core, y, 7 - z),
    ]
    sibling = partners[2]

    def partner(t):
        a, b = partners[0]
        for k in range(1, DEPTH):
            a, b = jnp.where(t == k + 1, partners[k][0], a), jnp.where(t == k + 1, partners[k][1], b)
        return a, b

    def role(t):
        return jnp.where(t == 0, 0, (me >> jnp.maximum(t - 1, 0)) % 2)

    def near_side(t):
        return jnp.where(role(t) == role(t + 1), 1, 0)

    barrier = pltpu.get_barrier_semaphore()
    for to in partners:
        pl.semaphore_signal(barrier, inc=1, device_id=to, device_id_type=pl.DeviceIdType.MESH)

    def piece(side, t, c, half):
        rows, col, cols = PARTS[c]
        start = half * rows if isinstance(half, int) else pl.multiple_of(half * rows, rows)
        return el.at[side, t, pl.ds(start, rows), pl.ds(col, cols)]

    def direct(t, c, half):
        return pltpu.make_async_remote_copy(
            src_ref=piece(0, t, c, half),
            dst_ref=piece(1, t, c, half),
            send_sem=send_sem.at[t, c, half],
            recv_sem=recv_sem.at[t, c, half],
            device_id=partner(t),
            device_id_type=pl.DeviceIdType.MESH,
        )

    def passed(t, c, half):
        return pltpu.make_async_remote_copy(
            src_ref=piece(1, t, c, half),
            dst_ref=piece(1, t, c, half),
            send_sem=pass_sem.at[t, c],
            recv_sem=recv_sem.at[t, c, half],
            device_id=sibling,
            device_id_type=pl.DeviceIdType.MESH,
        )

    def send(t, *parts):
        @pl.when(t <= DIRECT)
        def _():
            for c in parts:
                direct(t, c, 0).start()
                direct(t, c, 1).start()

        @pl.when((t > DIRECT) & (t <= DEPTH))
        def _():
            for c in parts:
                direct(t, c, core).start()

    def hand_on(t, *parts):
        @pl.when(t > DIRECT)
        def _():
            for c in parts:
                direct(t, c, core).wait_recv()
                passed(t, c, core).start()

    def receive(t, *parts):
        @pl.when((t > 0) & (t <= DIRECT))
        def _():
            for c in parts:
                direct(t, c, 0).wait_recv()
                direct(t, c, 1).wait_recv()

        @pl.when(t > DIRECT)
        def _():
            for c in parts:
                passed(t, c, 1 - core).wait_recv()

    zero = jnp.zeros((N, N), F32)
    is_first, is_last = me == 0, me == last
    f1 = jnp.where(is_first, zero, f[0])
    f2 = f[1]
    p1, p2 = p[0:1, :], p[1:2, :]
    p2_column = column_from(p2)
    weight = jnp.where(is_last, p2_column / (1.0 + p2_column), jnp.ones_like(p2_column))
    el[0, 0, :, :M0] = diag_of(1.0 + p1)
    el[1, 0, :, :M0] = mul_tn(f2, f2 * weight)
    el[0, 0, :, M0:C0] = -f1
    el[1, 0, :, M0:C0] = jnp.where(is_last, zero, -f2.T)
    el[0, 0, :, C0:O0] = info[0]
    tail = mul_tn(f2, info[1] / (1.0 + p2_column))
    el[1, 0, :, C0:O0] = jnp.where(is_last, tail, jnp.zeros_like(tail))
    el[0, 0, :, O0:E0] = mul_tn(f1, f1)
    el[1, 0, :, O0:E0] = diag_of(jnp.where(is_last, jnp.ones_like(p2), 1.0 + p2))
    el[0, 0, :, E0:] = jnp.zeros((N, RHS), F32)
    el[1, 0, :, E0:] = jnp.where(is_last, jnp.zeros_like(tail), info[1])
    pl.semaphore_wait(barrier, DEPTH)

    def merge(t, _):
        near = near_side(t)
        far = 1 - near
        hand_on(t, 0)
        receive(t, 0)
        x11 = inverse_half(el[0, t, :H, :H] + el[1, t, :H, :H], lambda: hand_on(t, 1))
        receive(t, 1)
        right = el[0, t, :, H:M0] + el[1, t, :, H:M0]
        a12, a22 = right[:H], right[H:]
        w = mul(x11, a12)
        y = inverse_half(a22 - mul_tn(a12, w), lambda: hand_on(t, 2))
        wy = mul(w, y)
        inv[:H, :H] = x11 + mul_nt(wy, w)
        inv[:H, H:] = -wy
        inv[H:, :H] = -mul_nt(y, w)
        inv[H:, H:] = y
        receive(t, 2)

        @pl.when(t < DEPTH)
        def _():
            hand_on(t, 3, 4)
            vb[t, near] = mul(inv[...], el[near, t, :, M0:C0])
            receive(t, 3, 4)
            g = el[near, t, :, M0:C0]
            el[0, t + 1, :, :M0] = el[near, t, :, O0:E0] - mul_tn(g, vb[t, near])
            send(t + 1, 0, 1)

        vb[t, far] = mul(inv[...], el[far, t, :, M0:C0])
        vs[t] = mul(inv[...], el[0, t, :, C0:O0] + el[1, t, :, C0:O0])

        @pl.when(t < DEPTH)
        def _():
            g = el[near, t, :, M0:C0]
            el[0, t + 1, :, M0:C0] = -mul_tn(g, vb[t, far])
            el[0, t + 1, :, C0:O0] = el[near, t, :, E0:] - mul_tn(g, vs[t])
            send(t + 1, 2)

        @pl.when(t < DEPTH - 1)
        def _():
            g = el[far, t, :, M0:C0]
            el[0, t + 1, :, O0:E0] = el[far, t, :, O0:E0] - mul_tn(g, vb[t, far])
            el[0, t + 1, :, E0:] = el[far, t, :, E0:] - mul_tn(g, vs[t])
            send(t + 1, 3, 4)

        @pl.when(t == DEPTH)
        def _():
            vb[t, near] = jnp.zeros((N, N), F32)

        return 0

    lax.fori_loop(0, DEPTH + 1, merge, 0)

    ends[...] = jnp.zeros((2, N, RHS), F32)

    def back(k, _):
        t = DEPTH - k
        o = ends[0]
        b = vs[t] - mul(vb[t, 0], o) - mul(vb[t, 1], ends[1])
        near = near_side(t - 1)
        ends[near] = b
        ends[1 - near] = o
        return 0

    lax.fori_loop(0, DEPTH, back, 0)
    b = vs[0] - mul(vb[0, 0], ends[0]) - mul(vb[0, 1], ends[1])
    out[0] = b
    end = (info[1] + mul(f2, b)) / (1.0 + p2_column)
    out[1] = jnp.where(is_last, end, ends[1])

    def finish(k, _):
        t = k + 1
        for c in range(len(PARTS)):
            if c < 3:
                used = t <= DEPTH
            else:
                used = t < DEPTH

            @pl.when(t <= DIRECT)
            def _():
                direct(t, c, 0).wait_send()
                direct(t, c, 1).wait_send()

            @pl.when((t > DIRECT) & used)
            def _():
                direct(t, c, core).wait_send()
                passed(t, c, core).wait_send()

        return 0

    lax.fori_loop(0, DEPTH, finish, 0)


VMEM = pl.BlockSpec(memory_space=pltpu.VMEM)


def shards(transition, precision, info):
    levels = DEPTH + 1
    return pl.pallas_call(
        kernel,
        out_shape=jax.ShapeDtypeStruct((2, N, RHS), F32),
        in_specs=[VMEM, VMEM, VMEM],
        out_specs=VMEM,
        scratch_shapes=[
            pltpu.VMEM((2, levels, N, WIDE), F32),
            pltpu.VMEM((levels, 2, N, N), F32),
            pltpu.VMEM((levels, N, RHS), F32),
            pltpu.VMEM((2, N, RHS), F32),
            pltpu.VMEM((N, N), F32),
            pltpu.SemaphoreType.DMA((levels, len(PARTS), 2)),
            pltpu.SemaphoreType.DMA((levels, len(PARTS), 2)),
            pltpu.SemaphoreType.DMA((levels, len(PARTS))),
        ],
        compiler_params=pltpu.CompilerParams(
            collective_id=0, has_side_effects=True, vmem_limit_bytes=48 * 1024 * 1024
        ),
        name="smooth",
    )(transition, precision, info)


def solution(mesh):
    placed = (P(("tm", "sub"), None, None), P(("tm", "sub"), None), P(("tm", "sub"), None, None))
    return jax.shard_map(
        shards, mesh=mesh, in_specs=placed, out_specs=P(("tm", "sub"), None, None), check_vma=False
    )
```

```python
import jax
import jax.numpy as jnp
from jax import lax
from jax.experimental import pallas as pl
from jax.experimental.pallas import tpu as pltpu
from jax.sharding import PartitionSpec as P

HIGHEST, HIGH = lax.Precision.HIGHEST, lax.Precision.HIGH
F32 = jnp.float32
N = 256
H = 128
RHS = 128
DEPTH = 8
DIRECT = 3
COARSE = 4
CHAIN = 7
M0, C0, O0, E0, WIDE = N, 2 * N, 2 * N + RHS, 3 * N + RHS, 4 * N
PARTS = ((64, 0, H), (128, H, H), (128, M0, N + RHS), (64, O0, H), (128, O0 + H, H + RHS), (128, C0, RHS))


def mul(a, b, precision=HIGHEST):
    return jnp.dot(a, b, precision=precision, preferred_element_type=F32)


def mul_tn(a, b, precision=HIGHEST):
    return lax.dot_general(a, b, (((0,), (0,)), ((), ())), precision=precision, preferred_element_type=F32)


def mul_nt(a, b, precision=HIGHEST):
    return lax.dot_general(a, b, (((1,), (1,)), ((), ())), precision=precision, preferred_element_type=F32)


def eliminate_panel(panel, base, lane, sub):
    cols = [jnp.broadcast_to(panel[:, base + j : base + j + 1], (8, H)) for j in range(8)]
    panel = jnp.where((lane >= base) & (lane < base + 8), jnp.where(lane - base == sub, 1.0, 0.0), panel)
    for s in (0, 2, 4, 6):
        x, y = cols[0], cols[1]
        a, b, d = (jnp.broadcast_to(q[i : i + 1, :], (8, H)) for q, i in ((x, s), (y, s), (y, s + 1)))
        r = 1.0 / (a * d - b * b)
        first, pair = sub == s, (sub == s) | (sub == s + 1)
        u = jnp.where(pair, jnp.where(first, d, -b), y * b - x * d) * r
        w = jnp.where(pair, jnp.where(first, -b, a), x * b - y * a) * r
        m = 7 - s
        wide = jnp.concatenate(cols[2:] + [panel], 1)
        q0 = jnp.broadcast_to(wide[s : s + 1, :], wide.shape)
        q1 = jnp.broadcast_to(wide[s + 1 : s + 2, :], wide.shape)
        keep = jnp.where(pair, 0.0, 1.0)
        keep, u, w = (jnp.concatenate([z] * m, 1) for z in (keep, u, w))
        wide = keep * wide + (u * q0 + w * q1)
        cols = [wide[:, H * j : H * j + H] for j in range(m - 1)]
        panel = wide[:, H * (m - 1) :]
    return panel


def inverse_half(a, middle=None):
    lane = lax.broadcasted_iota(jnp.int32, (8, H), 1)
    sub = lax.broadcasted_iota(jnp.int32, (8, H), 0)
    lanes = lax.broadcasted_iota(jnp.int32, (H, H), 1)
    for k in range(H // 8):
        if k == 8 and middle is not None:
            middle()
        base = 8 * k
        panel = eliminate_panel(a[base : base + 8, :], base, lane, sub)
        m = [
            jnp.broadcast_to(a[:, base + j : base + j + 1], (H, H)) * jnp.broadcast_to(panel[j : j + 1, :], (H, H))
            for j in range(8)
        ]
        total = ((m[0] + m[1]) + (m[2] + m[3])) + ((m[4] + m[5]) + (m[6] + m[7]))
        new = jnp.where((lanes >= base) & (lanes < base + 8), 0.0, a) - total
        parts = ([new[:base, :]] if k else []) + [panel] + ([new[base + 8 :, :]] if k < H // 8 - 1 else [])
        a = jnp.concatenate(parts, 0)
    return a


def on_diagonal():
    return lax.broadcasted_iota(jnp.int32, (N, N), 0) == lax.broadcasted_iota(jnp.int32, (N, N), 1)


def diag_of(row):
    return jnp.where(on_diagonal(), jnp.broadcast_to(row, (N, N)), 0.0)


def column_from(row):
    return jnp.sum(diag_of(row), 1, keepdims=True)


def kernel(f, p, info, out, el, vb, vs, ends, inv, send_sem, recv_sem, pass_sem, chain_sem):
    tm, x = lax.axis_index("tm"), lax.axis_index("sub")
    me = tm * 4 + x
    core, y, z = tm % 2, (tm // 2) % 4, tm // 8
    last = 2 ** DEPTH - 1

    def place(x, core, y, z):
        return (z * 4 + y) * 2 + core, x

    def other(q):
        return q + 1 - 2 * (q % 2)

    partners = [
        place(other(x), core, y, z),
        place(3 - x, core, y, z),
        place(x, 1 - core, y, z),
        place(x, core, other(y), z),
        place(x, core, 3 - y, z),
        place(x, core, y, other(z)),
        place(x, core, y, z + 3 - 2 * (z % 4)),
        place(x, core, y, 7 - z),
    ]
    sibling = partners[2]
    buddy = partners[5]

    def inner(t):
        middle = ((z + 1) // 2) % 2
        return jnp.where(t < CHAIN, 1, jnp.where(t == CHAIN, middle, 1 - middle)) == 1

    def partner(t):
        a, b = partners[0]
        for k in range(1, DEPTH):
            a, b = jnp.where(t == k + 1, partners[k][0], a), jnp.where(t == k + 1, partners[k][1], b)
        return a, b

    def role(t):
        return jnp.where(t == 0, 0, (me >> jnp.maximum(t - 1, 0)) % 2)

    def near_side(t):
        return jnp.where(role(t) == role(t + 1), 1, 0)

    barrier = pltpu.get_barrier_semaphore()
    for to in partners:
        pl.semaphore_signal(barrier, inc=1, device_id=to, device_id_type=pl.DeviceIdType.MESH)

    def piece(side, t, c, half):
        rows, col, cols = PARTS[c]
        start = half * rows if isinstance(half, int) else pl.multiple_of(half * rows, rows)
        return el.at[side, t, pl.ds(start, rows), pl.ds(col, cols)]

    def direct(t, c, half):
        return pltpu.make_async_remote_copy(
            src_ref=piece(0, t, c, half),
            dst_ref=piece(1, t, c, half),
            send_sem=send_sem.at[t, c, half],
            recv_sem=recv_sem.at[t, c, half],
            device_id=partner(t),
            device_id_type=pl.DeviceIdType.MESH,
        )

    def passed(t, c, half):
        return pltpu.make_async_remote_copy(
            src_ref=piece(1, t, c, half),
            dst_ref=piece(1, t, c, half),
            send_sem=pass_sem.at[t, c],
            recv_sem=recv_sem.at[t, c, half],
            device_id=sibling,
            device_id_type=pl.DeviceIdType.MESH,
        )

    def chained(t, c, half):
        return pltpu.make_async_remote_copy(
            src_ref=piece(1, t, c, half),
            dst_ref=piece(1, t, c, half),
            send_sem=chain_sem.at[t, c],
            recv_sem=recv_sem.at[t, c, half],
            device_id=buddy,
            device_id_type=pl.DeviceIdType.MESH,
        )

    def send(t, *parts):
        @pl.when(t <= DIRECT)
        def _():
            for c in parts:
                direct(t, c, 0).start()
                direct(t, c, 1).start()

        @pl.when((t > DIRECT) & inner(t))
        def _():
            for c in parts:
                direct(t, c, core).start()

    def hand_on(t, *parts):
        @pl.when(t > DIRECT)
        def _():
            for c in parts:
                direct(t, c, core).wait_recv()
                passed(t, c, core).start()

                @pl.when((t >= CHAIN) & inner(t))
                def _():
                    chained(t, c, core).start()

    def receive(t, *parts):
        @pl.when((t > 0) & (t <= DIRECT))
        def _():
            for c in parts:
                direct(t, c, 0).wait_recv()
                direct(t, c, 1).wait_recv()

        @pl.when(t > DIRECT)
        def _():
            for c in parts:
                passed(t, c, 1 - core).wait_recv()

    zero = jnp.zeros((N, N), F32)
    is_first, is_last = me == 0, me == last
    f1 = jnp.where(is_first, zero, f[0])
    f2 = f[1]
    p1, p2 = p[0:1, :], p[1:2, :]
    el[0, 0, :, :M0] = diag_of(1.0 + p1)
    el[0, 0, :, M0:C0] = -f1
    el[0, 0, :, C0:O0] = info[0]
    el[0, 0, :, O0:E0] = mul_tn(f1, f1)
    el[0, 0, :, E0:] = jnp.zeros((N, RHS), F32)

    @pl.when(jnp.logical_not(is_last))
    def _():
        el[1, 0, :, :M0] = mul_tn(f2, f2)
        el[1, 0, :, M0:C0] = -f2.T
        el[1, 0, :, C0:O0] = jnp.zeros((N, RHS), F32)
        el[1, 0, :, O0:E0] = diag_of(1.0 + p2)
        el[1, 0, :, E0:] = info[1]

    @pl.when(is_last)
    def _():
        p2_column = column_from(p2)
        el[1, 0, :, :M0] = mul_tn(f2, f2 * (p2_column / (1.0 + p2_column)))
        el[1, 0, :, M0:C0] = zero
        el[1, 0, :, C0:O0] = mul_tn(f2, info[1] / (1.0 + p2_column))
        el[1, 0, :, O0:E0] = diag_of(jnp.ones_like(p2))
        el[1, 0, :, E0:] = jnp.zeros((N, RHS), F32)

    pl.semaphore_wait(barrier, DEPTH)

    def merge(t, _):
        near = near_side(t)
        far = 1 - near

        def hand_on_coupling():
            @pl.when(t < DEPTH)
            def _():
                hand_on(t, 2)

            @pl.when(t == DEPTH)
            def _():
                hand_on(t, 5)

        hand_on(t, 0)
        receive(t, 0)
        x11 = inverse_half(el[0, t, :H, :H] + el[1, t, :H, :H], lambda: hand_on(t, 1))
        receive(t, 1)
        right = el[0, t, :, H:M0] + el[1, t, :, H:M0]
        a12, a22 = right[:H], right[H:]
        def by_level(step):
            @pl.when(t < COARSE)
            def _():
                step(HIGHEST)

            @pl.when(t >= COARSE)
            def _():
                step(HIGH)

        def complement(precision):
            w = mul(x11, a12, precision)
            inv[:H, H:] = w
            inv[H:, H:] = a22 - mul_tn(a12, w, precision)

        by_level(complement)
        y = inverse_half(inv[H:, H:], hand_on_coupling)

        def finish_level(precision):
            w = inv[:H, H:]
            wy = mul(w, y, precision)
            inv[:H, :H] = x11 + mul_nt(wy, w, precision)
            inv[:H, H:] = -wy
            inv[H:, :H] = -mul_nt(y, w, precision)
            inv[H:, H:] = y

            @pl.when(t < DEPTH)
            def _():
                receive(t, 2)
                hand_on(t, 3, 4)
                vb[t, near] = mul(inv[...], el[near, t, :, M0:C0], precision)
                receive(t, 3, 4)
                g = el[near, t, :, M0:C0]
                el[0, t + 1, :, :M0] = el[near, t, :, O0:E0] - mul_tn(g, vb[t, near], precision)
                send(t + 1, 0, 1)
                vs[t] = mul(inv[...], el[0, t, :, C0:O0] + el[1, t, :, C0:O0], precision)
                el[0, t + 1, :, C0:O0] = el[near, t, :, E0:] - mul_tn(g, vs[t], precision)
                vb[t, far] = mul(inv[...], el[far, t, :, M0:C0], precision)

            @pl.when(t == DEPTH - 1)
            def _():
                send(t + 1, 5)

            @pl.when(t < DEPTH - 1)
            def _():
                g = el[near, t, :, M0:C0]
                el[0, t + 1, :, M0:C0] = -mul_tn(g, vb[t, far], precision)
                send(t + 1, 2)
                g = el[far, t, :, M0:C0]
                el[0, t + 1, :, O0:E0] = el[far, t, :, O0:E0] - mul_tn(g, vb[t, far], precision)
                el[0, t + 1, :, E0:] = el[far, t, :, E0:] - mul_tn(g, vs[t], precision)
                send(t + 1, 3, 4)

            @pl.when(t == DEPTH)
            def _():
                receive(t, 5)
                vs[t] = mul(inv[...], el[0, t, :, C0:O0] + el[1, t, :, C0:O0], precision)

        by_level(finish_level)
        return 0

    lax.fori_loop(0, DEPTH + 1, merge, 0)

    near = near_side(DEPTH - 1)
    ends[near] = vs[DEPTH]
    ends[1 - near] = jnp.zeros((N, RHS), F32)

    def back(k, _):
        t = DEPTH - 1 - k
        o = ends[0]
        b = vs[t] - mul(vb[t, 0], o, HIGH) - mul(vb[t, 1], ends[1], HIGH)
        near = near_side(t - 1)
        ends[near] = b
        ends[1 - near] = o
        return 0

    lax.fori_loop(0, DEPTH - 1, back, 0)
    b = vs[0] - mul(vb[0, 0], ends[0], HIGH) - mul(vb[0, 1], ends[1], HIGH)
    out[0] = b

    @pl.when(jnp.logical_not(is_last))
    def _():
        out[1] = ends[1]

    @pl.when(is_last)
    def _():
        out[1] = (info[1] + mul(f2, b)) / (1.0 + column_from(p2))

    def finish(k, _):
        t = k + 1
        for c in range(len(PARTS)):
            used = {0: t > 0, 1: t > 0, 5: t == DEPTH}.get(c, t < DEPTH)

            @pl.when((t <= DIRECT) & used)
            def _():
                direct(t, c, 0).wait_send()
                direct(t, c, 1).wait_send()

            @pl.when((t > DIRECT) & used)
            def _():
                passed(t, c, core).wait_send()

            @pl.when((t > DIRECT) & used & inner(t))
            def _():
                direct(t, c, core).wait_send()

            @pl.when((t >= CHAIN) & used & inner(t))
            def _():
                chained(t, c, core).wait_send()

        return 0

    lax.fori_loop(0, DEPTH, finish, 0)


VMEM = pl.BlockSpec(memory_space=pltpu.VMEM)


def shards(transition, precision, info):
    levels = DEPTH + 1
    return pl.pallas_call(
        kernel,
        out_shape=jax.ShapeDtypeStruct((2, N, RHS), F32),
        in_specs=[VMEM, VMEM, VMEM],
        out_specs=VMEM,
        scratch_shapes=[
            pltpu.VMEM((2, levels, N, WIDE), F32),
            pltpu.VMEM((levels, 2, N, N), F32),
            pltpu.VMEM((levels, N, RHS), F32),
            pltpu.VMEM((2, N, RHS), F32),
            pltpu.VMEM((N, N), F32),
            pltpu.SemaphoreType.DMA((levels, len(PARTS), 2)),
            pltpu.SemaphoreType.DMA((levels, len(PARTS), 2)),
            pltpu.SemaphoreType.DMA((levels, len(PARTS))),
            pltpu.SemaphoreType.DMA((levels, len(PARTS))),
        ],
        compiler_params=pltpu.CompilerParams(
            collective_id=0, has_side_effects=True, vmem_limit_bytes=48 * 1024 * 1024
        ),
        name="smooth",
    )(transition, precision, info)


def solution(mesh):
    placed = (P(("tm", "sub"), None, None), P(("tm", "sub"), None), P(("tm", "sub"), None, None))
    return jax.shard_map(
        shards, mesh=mesh, in_specs=placed, out_specs=P(("tm", "sub"), None, None), check_vma=False
    )
```

```python
import jax
import jax.numpy as jnp
from jax import lax
from jax.experimental import pallas as pl
from jax.experimental.pallas import tpu as pltpu
from jax.sharding import PartitionSpec as P

HIGHEST, HIGH = lax.Precision.HIGHEST, lax.Precision.HIGH
F32 = jnp.float32
N = 256
H = 128
RHS = 128
DEPTH = 8
DIRECT = 3
COARSE = 4
CHAIN = 7
M0, C0, O0, E0, WIDE = N, 2 * N, 2 * N + RHS, 3 * N + RHS, 4 * N
PARTS = ((64, 0, H), (128, H, H), (128, M0, N + RHS), (64, O0, H), (128, O0 + H, H + RHS), (128, C0, RHS))


def mul(a, b, precision=HIGHEST):
    return jnp.dot(a, b, precision=precision, preferred_element_type=F32)


def mul_tn(a, b, precision=HIGHEST):
    return lax.dot_general(a, b, (((0,), (0,)), ((), ())), precision=precision, preferred_element_type=F32)


def mul_nt(a, b, precision=HIGHEST):
    return lax.dot_general(a, b, (((1,), (1,)), ((), ())), precision=precision, preferred_element_type=F32)


def eliminate_panel(panel, base, lane, sub):
    cols = [jnp.broadcast_to(panel[:, base + j : base + j + 1], (8, H)) for j in range(8)]
    panel = jnp.where((lane >= base) & (lane < base + 8), jnp.where(lane - base == sub, 1.0, 0.0), panel)
    for s in (0, 2, 4, 6):
        x, y = cols[0], cols[1]
        a, b, d = (jnp.broadcast_to(q[i : i + 1, :], (8, H)) for q, i in ((x, s), (y, s), (y, s + 1)))
        r = 1.0 / (a * d - b * b)
        first, pair = sub == s, (sub == s) | (sub == s + 1)
        u = jnp.where(pair, jnp.where(first, d, -b), y * b - x * d) * r
        w = jnp.where(pair, jnp.where(first, -b, a), x * b - y * a) * r
        m = 7 - s
        wide = jnp.concatenate(cols[2:] + [panel], 1)
        q0 = jnp.broadcast_to(wide[s : s + 1, :], wide.shape)
        q1 = jnp.broadcast_to(wide[s + 1 : s + 2, :], wide.shape)
        keep = jnp.where(pair, 0.0, 1.0)
        keep, u, w = (jnp.concatenate([z] * m, 1) for z in (keep, u, w))
        wide = keep * wide + (u * q0 + w * q1)
        cols = [wide[:, H * j : H * j + H] for j in range(m - 1)]
        panel = wide[:, H * (m - 1) :]
    return panel


def inverse_half(a, middle=None):
    lane = lax.broadcasted_iota(jnp.int32, (8, H), 1)
    sub = lax.broadcasted_iota(jnp.int32, (8, H), 0)
    lanes = lax.broadcasted_iota(jnp.int32, (H, H), 1)
    for k in range(H // 8):
        if k == 8 and middle is not None:
            middle()
        base = 8 * k
        panel = eliminate_panel(a[base : base + 8, :], base, lane, sub)
        m = [
            jnp.broadcast_to(a[:, base + j : base + j + 1], (H, H)) * jnp.broadcast_to(panel[j : j + 1, :], (H, H))
            for j in range(8)
        ]
        total = ((m[0] + m[1]) + (m[2] + m[3])) + ((m[4] + m[5]) + (m[6] + m[7]))
        new = jnp.where((lanes >= base) & (lanes < base + 8), 0.0, a) - total
        parts = ([new[:base, :]] if k else []) + [panel] + ([new[base + 8 :, :]] if k < H // 8 - 1 else [])
        a = jnp.concatenate(parts, 0)
    return a


def on_diagonal():
    return lax.broadcasted_iota(jnp.int32, (N, N), 0) == lax.broadcasted_iota(jnp.int32, (N, N), 1)


def diag_of(row):
    return jnp.where(on_diagonal(), jnp.broadcast_to(row, (N, N)), 0.0)


def column_from(row):
    return jnp.sum(diag_of(row), 1, keepdims=True)


def kernel(f, p, info, out, el, vb, vs, ends, inv, send_sem, recv_sem, pass_sem, chain_sem):
    tm, x = lax.axis_index("tm"), lax.axis_index("sub")
    me = tm * 4 + x
    core, y, z = tm % 2, (tm // 2) % 4, tm // 8
    last = 2 ** DEPTH - 1

    def place(x, core, y, z):
        return (z * 4 + y) * 2 + core, x

    def other(q):
        return q + 1 - 2 * (q % 2)

    partners = [
        place(other(x), core, y, z),
        place(3 - x, core, y, z),
        place(x, 1 - core, y, z),
        place(x, core, other(y), z),
        place(x, core, 3 - y, z),
        place(x, core, y, other(z)),
        place(x, core, y, z + 3 - 2 * (z % 4)),
        place(x, core, y, 7 - z),
    ]
    sibling = partners[2]
    buddy = partners[5]

    def inner(t):
        middle = ((z + 1) // 2) % 2
        return jnp.where(t < CHAIN, 1, jnp.where(t == CHAIN, middle, 1 - middle)) == 1

    def partner(t):
        a, b = partners[0]
        for k in range(1, DEPTH):
            a, b = jnp.where(t == k + 1, partners[k][0], a), jnp.where(t == k + 1, partners[k][1], b)
        return a, b

    def role(t):
        return jnp.where(t == 0, 0, (me >> jnp.maximum(t - 1, 0)) % 2)

    def near_side(t):
        return jnp.where(role(t) == role(t + 1), 1, 0)

    barrier = pltpu.get_barrier_semaphore()
    for to in partners:
        pl.semaphore_signal(barrier, inc=1, device_id=to, device_id_type=pl.DeviceIdType.MESH)

    def piece(side, t, c, half):
        rows, col, cols = PARTS[c]
        start = half * rows if isinstance(half, int) else pl.multiple_of(half * rows, rows)
        return el.at[side, t, pl.ds(start, rows), pl.ds(col, cols)]

    def direct(t, c, half):
        return pltpu.make_async_remote_copy(
            src_ref=piece(0, t, c, half),
            dst_ref=piece(1, t, c, half),
            send_sem=send_sem.at[t, c, half],
            recv_sem=recv_sem.at[t, c, half],
            device_id=partner(t),
            device_id_type=pl.DeviceIdType.MESH,
        )

    def passed(t, c, half):
        return pltpu.make_async_remote_copy(
            src_ref=piece(1, t, c, half),
            dst_ref=piece(1, t, c, half),
            send_sem=pass_sem.at[t, c],
            recv_sem=recv_sem.at[t, c, half],
            device_id=sibling,
            device_id_type=pl.DeviceIdType.MESH,
        )

    def chained(t, c, half):
        return pltpu.make_async_remote_copy(
            src_ref=piece(1, t, c, half),
            dst_ref=piece(1, t, c, half),
            send_sem=chain_sem.at[t, c],
            recv_sem=recv_sem.at[t, c, half],
            device_id=buddy,
            device_id_type=pl.DeviceIdType.MESH,
        )

    def send(t, *parts):
        @pl.when(t <= DIRECT)
        def _():
            for c in parts:
                direct(t, c, 0).start()
                direct(t, c, 1).start()

        @pl.when((t > DIRECT) & inner(t))
        def _():
            for c in parts:
                direct(t, c, core).start()

    def hand_on(t, *parts):
        @pl.when(t > DIRECT)
        def _():
            for c in parts:
                direct(t, c, core).wait_recv()
                passed(t, c, core).start()

                @pl.when((t >= CHAIN) & inner(t))
                def _():
                    chained(t, c, core).start()

    def receive(t, *parts):
        @pl.when((t > 0) & (t <= DIRECT))
        def _():
            for c in parts:
                direct(t, c, 0).wait_recv()
                direct(t, c, 1).wait_recv()

        @pl.when(t > DIRECT)
        def _():
            for c in parts:
                passed(t, c, 1 - core).wait_recv()

    zero = jnp.zeros((N, N), F32)
    is_first, is_last = me == 0, me == last
    f1 = jnp.where(is_first, zero, f[0])
    f2 = f[1]
    p1, p2 = p[0:1, :], p[1:2, :]
    el[0, 0, :, :M0] = diag_of(1.0 + p1)
    el[0, 0, :, M0:C0] = -f1
    el[0, 0, :, C0:O0] = info[0]
    el[0, 0, :, O0:E0] = mul_tn(f1, f1)
    el[0, 0, :, E0:] = jnp.zeros((N, RHS), F32)

    @pl.when(jnp.logical_not(is_last))
    def _():
        el[1, 0, :, :M0] = mul_tn(f2, f2)
        el[1, 0, :, M0:C0] = -f2.T
        el[1, 0, :, C0:O0] = jnp.zeros((N, RHS), F32)
        el[1, 0, :, O0:E0] = diag_of(1.0 + p2)
        el[1, 0, :, E0:] = info[1]

    @pl.when(is_last)
    def _():
        p2_column = column_from(p2)
        el[1, 0, :, :M0] = mul_tn(f2, f2 * (p2_column / (1.0 + p2_column)))
        el[1, 0, :, M0:C0] = zero
        el[1, 0, :, C0:O0] = mul_tn(f2, info[1] / (1.0 + p2_column))
        el[1, 0, :, O0:E0] = diag_of(jnp.ones_like(p2))
        el[1, 0, :, E0:] = jnp.zeros((N, RHS), F32)

    pl.semaphore_wait(barrier, DEPTH)

    def merge(t, _):
        near = near_side(t)
        far = 1 - near

        def hand_on_coupling():
            @pl.when(t < DEPTH)
            def _():
                hand_on(t, 2)

            @pl.when(t == DEPTH)
            def _():
                hand_on(t, 5)

        hand_on(t, 0)
        receive(t, 0)
        x11 = inverse_half(el[0, t, :H, :H] + el[1, t, :H, :H], lambda: hand_on(t, 1))
        receive(t, 1)
        right = el[0, t, :, H:M0] + el[1, t, :, H:M0]
        a12, a22 = right[:H], right[H:]
        def by_level(step):
            @pl.when(t < COARSE)
            def _():
                step(HIGHEST)

            @pl.when(t >= COARSE)
            def _():
                step(HIGH)

        def complement(precision):
            w = mul(x11, a12, precision)
            inv[:H, H:] = w
            inv[H:, H:] = a22 - mul_tn(a12, w, precision)

        by_level(complement)
        y = inverse_half(inv[H:, H:], hand_on_coupling)

        def finish_level(precision):
            w = inv[:H, H:]
            wy = mul(w, y, precision)
            inv[:H, :H] = x11 + mul_nt(wy, w, precision)
            inv[:H, H:] = -wy
            inv[H:, :H] = -mul_nt(y, w, precision)
            inv[H:, H:] = y

            @pl.when(t < DEPTH)
            def _():
                receive(t, 2)
                hand_on(t, 3, 4)
                vb[t, near] = mul(inv[...], el[near, t, :, M0:C0], precision)
                g = el[near, t, :, M0:C0]
                product = mul_tn(g, vb[t, near], precision)
                receive(t, 3, 4)
                el[0, t + 1, :, :M0] = el[near, t, :, O0:E0] - product
                send(t + 1, 0, 1)
                vs[t] = mul(inv[...], el[0, t, :, C0:O0] + el[1, t, :, C0:O0], precision)
                el[0, t + 1, :, C0:O0] = el[near, t, :, E0:] - mul_tn(g, vs[t], precision)
                vb[t, far] = mul(inv[...], el[far, t, :, M0:C0], precision)

            @pl.when(t == DEPTH - 1)
            def _():
                send(t + 1, 5)

            @pl.when(t < DEPTH - 1)
            def _():
                g = el[near, t, :, M0:C0]
                el[0, t + 1, :, M0:C0] = -mul_tn(g, vb[t, far], precision)
                send(t + 1, 2)
                g = el[far, t, :, M0:C0]
                el[0, t + 1, :, O0:E0] = el[far, t, :, O0:E0] - mul_tn(g, vb[t, far], precision)
                el[0, t + 1, :, E0:] = el[far, t, :, E0:] - mul_tn(g, vs[t], precision)
                send(t + 1, 3, 4)

            @pl.when(t == DEPTH)
            def _():
                receive(t, 5)
                vs[t] = mul(inv[...], el[0, t, :, C0:O0] + el[1, t, :, C0:O0], precision)

        by_level(finish_level)
        return 0

    lax.fori_loop(0, DEPTH + 1, merge, 0)

    near = near_side(DEPTH - 1)
    ends[near] = vs[DEPTH]
    ends[1 - near] = jnp.zeros((N, RHS), F32)

    def back(k, _):
        t = DEPTH - 1 - k
        o = ends[0]
        b = vs[t] - mul(vb[t, 0], o, HIGH) - mul(vb[t, 1], ends[1], HIGH)
        near = near_side(t - 1)
        ends[near] = b
        ends[1 - near] = o
        return 0

    lax.fori_loop(0, DEPTH - 1, back, 0)
    b = vs[0] - mul(vb[0, 0], ends[0], HIGH) - mul(vb[0, 1], ends[1], HIGH)
    out[0] = b

    @pl.when(jnp.logical_not(is_last))
    def _():
        out[1] = ends[1]

    @pl.when(is_last)
    def _():
        out[1] = (info[1] + mul(f2, b)) / (1.0 + column_from(p2))

    def finish(k, _):
        t = k + 1
        for c in range(len(PARTS)):
            used = {0: t > 0, 1: t > 0, 5: t == DEPTH}.get(c, t < DEPTH)

            @pl.when((t <= DIRECT) & used)
            def _():
                direct(t, c, 0).wait_send()
                direct(t, c, 1).wait_send()

            @pl.when((t > DIRECT) & used)
            def _():
                passed(t, c, core).wait_send()

            @pl.when((t > DIRECT) & used & inner(t))
            def _():
                direct(t, c, core).wait_send()

            @pl.when((t >= CHAIN) & used & inner(t))
            def _():
                chained(t, c, core).wait_send()

        return 0

    lax.fori_loop(0, DEPTH, finish, 0)


VMEM = pl.BlockSpec(memory_space=pltpu.VMEM)


def shards(transition, precision, info):
    levels = DEPTH + 1
    return pl.pallas_call(
        kernel,
        out_shape=jax.ShapeDtypeStruct((2, N, RHS), F32),
        in_specs=[VMEM, VMEM, VMEM],
        out_specs=VMEM,
        scratch_shapes=[
            pltpu.VMEM((2, levels, N, WIDE), F32),
            pltpu.VMEM((levels, 2, N, N), F32),
            pltpu.VMEM((levels, N, RHS), F32),
            pltpu.VMEM((2, N, RHS), F32),
            pltpu.VMEM((N, N), F32),
            pltpu.SemaphoreType.DMA((levels, len(PARTS), 2)),
            pltpu.SemaphoreType.DMA((levels, len(PARTS), 2)),
            pltpu.SemaphoreType.DMA((levels, len(PARTS))),
            pltpu.SemaphoreType.DMA((levels, len(PARTS))),
        ],
        compiler_params=pltpu.CompilerParams(
            collective_id=0, has_side_effects=True, vmem_limit_bytes=48 * 1024 * 1024
        ),
        name="smooth",
    )(transition, precision, info)


def solution(mesh):
    placed = (P(("tm", "sub"), None, None), P(("tm", "sub"), None), P(("tm", "sub"), None, None))
    return jax.shard_map(
        shards, mesh=mesh, in_specs=placed, out_specs=P(("tm", "sub"), None, None), check_vma=False
    )
```

```python
import jax
import jax.numpy as jnp
from jax import lax
from jax.experimental import pallas as pl
from jax.experimental.pallas import tpu as pltpu
from jax.sharding import PartitionSpec as P

HIGHEST, HIGH = lax.Precision.HIGHEST, lax.Precision.HIGH
F32 = jnp.float32
N = 256
H = 128
RHS = 128
DEPTH = 8
DIRECT = 3
COARSE = 4
CHAIN = 7
M0, C0, O0, E0, WIDE = N, 2 * N, 2 * N + RHS, 3 * N + RHS, 4 * N
PARTS = ((64, 0, H), (128, H, H), (128, M0, N + RHS), (64, O0, H), (128, O0 + H, H + RHS), (128, C0, RHS))


def mul(a, b, precision=HIGHEST):
    return jnp.dot(a, b, precision=precision, preferred_element_type=F32)


def mul_tn(a, b, precision=HIGHEST):
    return lax.dot_general(a, b, (((0,), (0,)), ((), ())), precision=precision, preferred_element_type=F32)


def mul_nt(a, b, precision=HIGHEST):
    return lax.dot_general(a, b, (((1,), (1,)), ((), ())), precision=precision, preferred_element_type=F32)


def eliminate_panel(panel, base, lane, sub):
    cols = [jnp.broadcast_to(panel[:, base + j : base + j + 1], (8, H)) for j in range(8)]
    panel = jnp.where((lane >= base) & (lane < base + 8), jnp.where(lane - base == sub, 1.0, 0.0), panel)
    for s in (0, 2, 4, 6):
        x, y = cols[0], cols[1]
        a, b, d = (jnp.broadcast_to(q[i : i + 1, :], (8, H)) for q, i in ((x, s), (y, s), (y, s + 1)))
        r = 1.0 / (a * d - b * b)
        first, pair = sub == s, (sub == s) | (sub == s + 1)
        u = jnp.where(pair, jnp.where(first, d, -b), y * b - x * d) * r
        w = jnp.where(pair, jnp.where(first, -b, a), x * b - y * a) * r
        m = 7 - s
        wide = jnp.concatenate(cols[2:] + [panel], 1)
        q0 = jnp.broadcast_to(wide[s : s + 1, :], wide.shape)
        q1 = jnp.broadcast_to(wide[s + 1 : s + 2, :], wide.shape)
        keep = jnp.where(pair, 0.0, 1.0)
        keep, u, w = (jnp.concatenate([z] * m, 1) for z in (keep, u, w))
        wide = keep * wide + (u * q0 + w * q1)
        cols = [wide[:, H * j : H * j + H] for j in range(m - 1)]
        panel = wide[:, H * (m - 1) :]
    return panel


def inverse_half(a, middle=None):
    lane = lax.broadcasted_iota(jnp.int32, (8, H), 1)
    sub = lax.broadcasted_iota(jnp.int32, (8, H), 0)
    lanes = lax.broadcasted_iota(jnp.int32, (H, H), 1)
    for k in range(H // 8):
        if k == 8 and middle is not None:
            middle()
        base = 8 * k
        panel = eliminate_panel(a[base : base + 8, :], base, lane, sub)
        m = [
            jnp.broadcast_to(a[:, base + j : base + j + 1], (H, H)) * jnp.broadcast_to(panel[j : j + 1, :], (H, H))
            for j in range(8)
        ]
        total = ((m[0] + m[1]) + (m[2] + m[3])) + ((m[4] + m[5]) + (m[6] + m[7]))
        new = jnp.where((lanes >= base) & (lanes < base + 8), 0.0, a) - total
        parts = ([new[:base, :]] if k else []) + [panel] + ([new[base + 8 :, :]] if k < H // 8 - 1 else [])
        a = jnp.concatenate(parts, 0)
    return a


def on_diagonal():
    return lax.broadcasted_iota(jnp.int32, (N, N), 0) == lax.broadcasted_iota(jnp.int32, (N, N), 1)


def diag_of(row):
    return jnp.where(on_diagonal(), jnp.broadcast_to(row, (N, N)), 0.0)


def column_from(row):
    return jnp.sum(diag_of(row), 1, keepdims=True)


def kernel(f, p, info, out, el, vb, vs, ends, inv, send_sem, recv_sem, pass_sem, chain_sem):
    tm, x = lax.axis_index("tm"), lax.axis_index("sub")
    me = tm * 4 + x
    core, y, z = tm % 2, (tm // 2) % 4, tm // 8
    last = 2 ** DEPTH - 1

    def place(x, core, y, z):
        return (z * 4 + y) * 2 + core, x

    def other(q):
        return q + 1 - 2 * (q % 2)

    partners = [
        place(other(x), core, y, z),
        place(3 - x, core, y, z),
        place(x, 1 - core, y, z),
        place(x, core, other(y), z),
        place(x, core, 3 - y, z),
        place(x, core, y, other(z)),
        place(x, core, y, z + 3 - 2 * (z % 4)),
        place(x, core, y, 7 - z),
    ]
    sibling = partners[2]
    buddy = partners[5]

    def inner(t):
        middle = ((z + 1) // 2) % 2
        return jnp.where(t < CHAIN, 1, jnp.where(t == CHAIN, middle, 1 - middle)) == 1

    def partner(t):
        a, b = partners[0]
        for k in range(1, DEPTH):
            a, b = jnp.where(t == k + 1, partners[k][0], a), jnp.where(t == k + 1, partners[k][1], b)
        return a, b

    def role(t):
        return jnp.where(t == 0, 0, (me >> jnp.maximum(t - 1, 0)) % 2)

    def near_side(t):
        return jnp.where(role(t) == role(t + 1), 1, 0)

    barrier = pltpu.get_barrier_semaphore()
    for to in partners:
        pl.semaphore_signal(barrier, inc=1, device_id=to, device_id_type=pl.DeviceIdType.MESH)

    def piece(side, t, c, half):
        rows, col, cols = PARTS[c]
        start = half * rows if isinstance(half, int) else pl.multiple_of(half * rows, rows)
        return el.at[side, t, pl.ds(start, rows), pl.ds(col, cols)]

    def direct(t, c, half):
        return pltpu.make_async_remote_copy(
            src_ref=piece(0, t, c, half),
            dst_ref=piece(1, t, c, half),
            send_sem=send_sem.at[t, c, half],
            recv_sem=recv_sem.at[t, c, half],
            device_id=partner(t),
            device_id_type=pl.DeviceIdType.MESH,
        )

    def passed(t, c, half):
        return pltpu.make_async_remote_copy(
            src_ref=piece(1, t, c, half),
            dst_ref=piece(1, t, c, half),
            send_sem=pass_sem.at[t, c],
            recv_sem=recv_sem.at[t, c, half],
            device_id=sibling,
            device_id_type=pl.DeviceIdType.MESH,
        )

    def chained(t, c, half):
        return pltpu.make_async_remote_copy(
            src_ref=piece(1, t, c, half),
            dst_ref=piece(1, t, c, half),
            send_sem=chain_sem.at[t, c],
            recv_sem=recv_sem.at[t, c, half],
            device_id=buddy,
            device_id_type=pl.DeviceIdType.MESH,
        )

    def send(t, *parts):
        @pl.when(t <= DIRECT)
        def _():
            for c in parts:
                direct(t, c, 0).start()
                direct(t, c, 1).start()

        @pl.when((t > DIRECT) & inner(t))
        def _():
            for c in parts:
                direct(t, c, core).start()

    def hand_on(t, *parts):
        @pl.when(t > DIRECT)
        def _():
            for c in parts:
                direct(t, c, core).wait_recv()
                passed(t, c, core).start()

                @pl.when((t >= CHAIN) & inner(t))
                def _():
                    chained(t, c, core).start()

    def receive(t, *parts):
        @pl.when((t > 0) & (t <= DIRECT))
        def _():
            for c in parts:
                direct(t, c, 0).wait_recv()
                direct(t, c, 1).wait_recv()

        @pl.when(t > DIRECT)
        def _():
            for c in parts:
                passed(t, c, 1 - core).wait_recv()

    zero = jnp.zeros((N, N), F32)
    is_first, is_last = me == 0, me == last
    f1 = jnp.where(is_first, zero, f[0])
    f2 = f[1]
    p1, p2 = p[0:1, :], p[1:2, :]
    el[0, 0, :, :M0] = diag_of(1.0 + p1)
    el[0, 0, :, M0:C0] = -f1
    el[0, 0, :, C0:O0] = info[0]
    el[0, 0, :, O0:E0] = mul_tn(f1, f1)
    el[0, 0, :, E0:] = jnp.zeros((N, RHS), F32)

    @pl.when(jnp.logical_not(is_last))
    def _():
        el[1, 0, :, :M0] = mul_tn(f2, f2)
        el[1, 0, :, M0:C0] = -f2.T
        el[1, 0, :, C0:O0] = jnp.zeros((N, RHS), F32)
        el[1, 0, :, O0:E0] = diag_of(1.0 + p2)
        el[1, 0, :, E0:] = info[1]

    @pl.when(is_last)
    def _():
        p2_column = column_from(p2)
        el[1, 0, :, :M0] = mul_tn(f2, f2 * (p2_column / (1.0 + p2_column)))
        el[1, 0, :, M0:C0] = zero
        el[1, 0, :, C0:O0] = mul_tn(f2, info[1] / (1.0 + p2_column))
        el[1, 0, :, O0:E0] = diag_of(jnp.ones_like(p2))
        el[1, 0, :, E0:] = jnp.zeros((N, RHS), F32)

    pl.semaphore_wait(barrier, DEPTH)

    def merge(t, _):
        near = near_side(t)
        far = 1 - near

        def hand_on_coupling():
            @pl.when(t < DEPTH)
            def _():
                hand_on(t, 2)

            @pl.when(t == DEPTH)
            def _():
                hand_on(t, 5)

        hand_on(t, 0)
        receive(t, 0)
        x11 = inverse_half(el[0, t, :H, :H] + el[1, t, :H, :H], lambda: hand_on(t, 1))
        receive(t, 1)
        right = el[0, t, :, H:M0] + el[1, t, :, H:M0]
        a12, a22 = right[:H], right[H:]
        def by_level(step):
            @pl.when(t < COARSE)
            def _():
                step(HIGHEST)

            @pl.when(t >= COARSE)
            def _():
                step(HIGH)

        def complement(precision):
            w = mul(x11, a12, precision)
            inv[:H, H:] = w
            inv[H:, H:] = a22 - mul_tn(a12, w, precision)

        by_level(complement)
        y = inverse_half(inv[H:, H:], hand_on_coupling)

        def finish_level(precision):
            w = inv[:H, H:]
            wy = mul(w, y, precision)
            inv[:H, :H] = x11 + mul_nt(wy, w, precision)
            inv[:H, H:] = -wy
            inv[H:, :H] = -mul_nt(y, w, precision)
            inv[H:, H:] = y

            @pl.when(t < DEPTH)
            def _():
                receive(t, 2)
                hand_on(t, 3, 4)
                vb[t, near] = mul(inv[...], el[near, t, :, M0:C0], precision)
                g = el[near, t, :, M0:C0]
                upper = mul_tn(g[:, :H], vb[t, near], precision)
                lower = mul_tn(g[:, H:], vb[t, near, :, H:], precision)
                receive(t, 3, 4)
                el[0, t + 1, :H, :M0] = el[near, t, :H, O0:E0] - upper
                el[0, t + 1, H:, H:M0] = el[near, t, H:, O0 + H : E0] - lower
                send(t + 1, 0, 1)
                vs[t] = mul(inv[...], el[0, t, :, C0:O0] + el[1, t, :, C0:O0], precision)
                el[0, t + 1, :, C0:O0] = el[near, t, :, E0:] - mul_tn(g, vs[t], precision)
                vb[t, far] = mul(inv[...], el[far, t, :, M0:C0], precision)

            @pl.when(t == DEPTH - 1)
            def _():
                send(t + 1, 5)

            @pl.when(t < DEPTH - 1)
            def _():
                g = el[near, t, :, M0:C0]
                el[0, t + 1, :, M0:C0] = -mul_tn(g, vb[t, far], precision)
                send(t + 1, 2)
                g = el[far, t, :, M0:C0]
                el[0, t + 1, :, O0:E0] = el[far, t, :, O0:E0] - mul_tn(g, vb[t, far], precision)
                el[0, t + 1, :, E0:] = el[far, t, :, E0:] - mul_tn(g, vs[t], precision)
                send(t + 1, 3, 4)

            @pl.when(t == DEPTH)
            def _():
                receive(t, 5)
                vs[t] = mul(inv[...], el[0, t, :, C0:O0] + el[1, t, :, C0:O0], precision)

        by_level(finish_level)
        return 0

    lax.fori_loop(0, DEPTH + 1, merge, 0)

    near = near_side(DEPTH - 1)
    ends[near] = vs[DEPTH]
    ends[1 - near] = jnp.zeros((N, RHS), F32)

    def back(k, _):
        t = DEPTH - 1 - k
        o = ends[0]
        b = vs[t] - mul(vb[t, 0], o, HIGH) - mul(vb[t, 1], ends[1], HIGH)
        near = near_side(t - 1)
        ends[near] = b
        ends[1 - near] = o
        return 0

    lax.fori_loop(0, DEPTH - 1, back, 0)
    b = vs[0] - mul(vb[0, 0], ends[0], HIGH) - mul(vb[0, 1], ends[1], HIGH)
    out[0] = b

    @pl.when(jnp.logical_not(is_last))
    def _():
        out[1] = ends[1]

    @pl.when(is_last)
    def _():
        out[1] = (info[1] + mul(f2, b)) / (1.0 + column_from(p2))

    def finish(k, _):
        t = k + 1
        for c in range(len(PARTS)):
            used = {0: t > 0, 1: t > 0, 5: t == DEPTH}.get(c, t < DEPTH)

            @pl.when((t <= DIRECT) & used)
            def _():
                direct(t, c, 0).wait_send()
                direct(t, c, 1).wait_send()

            @pl.when((t > DIRECT) & used)
            def _():
                passed(t, c, core).wait_send()

            @pl.when((t > DIRECT) & used & inner(t))
            def _():
                direct(t, c, core).wait_send()

            @pl.when((t >= CHAIN) & used & inner(t))
            def _():
                chained(t, c, core).wait_send()

        return 0

    lax.fori_loop(0, DEPTH, finish, 0)


VMEM = pl.BlockSpec(memory_space=pltpu.VMEM)


def shards(transition, precision, info):
    levels = DEPTH + 1
    return pl.pallas_call(
        kernel,
        out_shape=jax.ShapeDtypeStruct((2, N, RHS), F32),
        in_specs=[VMEM, VMEM, VMEM],
        out_specs=VMEM,
        scratch_shapes=[
            pltpu.VMEM((2, levels, N, WIDE), F32),
            pltpu.VMEM((levels, 2, N, N), F32),
            pltpu.VMEM((levels, N, RHS), F32),
            pltpu.VMEM((2, N, RHS), F32),
            pltpu.VMEM((N, N), F32),
            pltpu.SemaphoreType.DMA((levels, len(PARTS), 2)),
            pltpu.SemaphoreType.DMA((levels, len(PARTS), 2)),
            pltpu.SemaphoreType.DMA((levels, len(PARTS))),
            pltpu.SemaphoreType.DMA((levels, len(PARTS))),
        ],
        compiler_params=pltpu.CompilerParams(
            collective_id=0, has_side_effects=True, vmem_limit_bytes=48 * 1024 * 1024
        ),
        name="smooth",
    )(transition, precision, info)


def solution(mesh):
    placed = (P(("tm", "sub"), None, None), P(("tm", "sub"), None), P(("tm", "sub"), None, None))
    return jax.shard_map(
        shards, mesh=mesh, in_specs=placed, out_specs=P(("tm", "sub"), None, None), check_vma=False
    )
```
